256 devices in a mesh: section: 8 (over y, z_lo), rows: 4 (over x), hid: 8 (over z_hi, core).
Axes of the slice: x: 4, y: 4, z: 8 (z_hi: 4, z_lo: 2; z = z_hi * 2 + z_lo), core: 2. Of those that a mesh axis runs over, the one named last changes fastest.
Arguments:
- acts: bfloat16 [8, 1024, 4096], P('section', 'rows', 'hid'), may hold values from -11 to 11
- ln_gain: float32 [8, 4096], P('section'), may hold values from 0.1 to 1.9
- ln_bias: float32 [8, 4096], P('section'), may hold values from -1.5 to 1.5
- w_up: bfloat16 [8, 4096, 16384], P('section', None, ('rows', 'hid')), may hold values from -0.09375 to 0.09375
- b_up: float32 [8, 16384], P('section', ('rows', 'hid')), may hold values from -3 to 3
- w_down: bfloat16 [8, 16384, 4096], P('section', ('rows', 'hid')), may hold values from -0.09375 to 0.09375
- b_down: float32 [8, 4096], P('section'), may hold values from -3 to 3
Outputs:
- arrived: bfloat16 [8, 2, 512, 4096], P('section', None, 'rows', 'hid')
The draws below stay inside these ranges and needn't reach their ends.
All inputs are finite; a program needn't handle non-finite values.
Results may differ from the reference program's by a relative error of at most 0.0041.
Values may be sent and summed in bfloat16 or wider, within the bound.
No kernel may reach another device: no remote copies, remote signals or barrier semaphores. Data moves between devices by JAX's collectives and lax.ppermute only.
A program may use at most 128 MiB of HBM per device.

```python
import math
import jax
import jax.numpy as jnp
from jax import lax

D = 4096
FFW = 16384
BATCH = 2
SEQ = 512
N_SECTION = 8


def draw_acts(key, part):
    key = jax.random.fold_in(key, 11)
    key_base, key_cols, key_rows = jax.random.split(key, 3)
    shape = (N_SECTION, BATCH * SEQ, D)
    cols = jnp.exp(jax.random.uniform(key_cols, (D,), jnp.float32, math.log(0.3), math.log(3.0)))
    rows = jnp.exp(jax.random.uniform(key_rows, (N_SECTION, BATCH * SEQ, 1), jnp.float32, math.log(0.6), math.log(1.2)))
    base = jax.random.truncated_normal(key_base, -3.0, 3.0, shape, jnp.float32)
    return (base * cols * rows).astype(jnp.bfloat16)


def raised(entries, stream_key, source, target, parts, factor):
    owner, partner = [(jnp.arange(entries.shape[axis_at]) // (entries.shape[axis_at] // parts)).reshape([-1 if axis == axis_at else 1 for axis in range(entries.ndim)]) for axis_at in (source, target)]
    chosen = jax.random.permutation(stream_key, parts)[partner]
    strong = (owner == chosen) | (owner == (partner + parts // 2) % parts)
    return jnp.where(strong, factor * entries, entries)


def level_of(key, dims, pieces, smallest, top_value):
    level, own = 1.0, jax.random.fold_in(key, 6)
    for dim, shards_of in pieces:
        heights = jnp.exp(jax.random.uniform(jax.random.fold_in(own, dim), (shards_of,), jnp.float32, smallest / len(pieces), top_value / len(pieces)))
        level = level * jnp.repeat(heights, dims[dim] // shards_of).reshape([-1 if axis == dim else 1 for axis in range(len(dims))])
    return level


def centred(own_key, extent, scale, limit, cuts=(), held_as=jnp.bfloat16):
    entries = jax.random.normal(own_key, extent, jnp.float32) * scale
    if len(cuts) > 0:
        entries = level_of(own_key, extent, cuts, -0.22, 0.18) * entries
    return jnp.clip(entries, min=-limit, max=limit).astype(held_as)


def noise_with(own_key, extent, deviation, most, pieces, heavy, kind=jnp.bfloat16):
    result = deviation * jax.random.normal(own_key, extent, jnp.float32)
    if pieces:
        result = result * level_of(own_key, extent, pieces, -0.22, 0.18)
    return jnp.clip(raised(result, jax.random.fold_in(own_key, 3), *heavy), -most, most).astype(kind)


def setup_inputs(seed: int = 0) -> dict:
    splits = jax.random.split(jax.random.key(seed), 8)
    acts = draw_acts(jax.random.fold_in(splits[7], 71), 0)
    ln_gain = jnp.clip(1.0 + 0.18 * jax.random.normal(splits[1], (N_SECTION, D), jnp.float32), 0.1, 1.9)
    ln_bias = centred(splits[2], (N_SECTION, D), 0.3, 1.5, ((0, 8),), jnp.float32)
    w_up = centred(splits[3], (N_SECTION, D, FFW), D ** -0.5, 0.09375, ((0, 8), (2, 32)))
    b_up = centred(splits[4], (N_SECTION, FFW), 0.5, 3.0, ((0, 8), (1, 32)), jnp.float32)
    w_down = noise_with(splits[5], (N_SECTION, FFW, D), FFW ** -0.5, 0.09375, ((0, 8), (1, 32)), (1, 2, 32, 2.75))
    b_down = centred(splits[6], (N_SECTION, D), 0.5, 3.0, ((0, 8),), jnp.float32)
    return {"acts": acts, "ln_gain": ln_gain, "ln_bias": ln_bias, "w_up": w_up, "b_up": b_up, "w_down": w_down, "b_down": b_down}


def run_section(items):
    acts_s, gain_s, bias_s, up_s, bup_s, down_s, bdown_s = items
    values = acts_s.astype(jnp.float32)
    mean = lax.optimization_barrier(jnp.mean(values, axis=-1, keepdims=True))
    centered = values - mean
    spread = lax.optimization_barrier(jnp.mean(centered * centered, axis=-1, keepdims=True))
    normed = (centered * lax.rsqrt(spread + 1e-05) * gain_s + bias_s).astype(jnp.bfloat16)
    pre = jnp.dot(normed, up_s, preferred_element_type=jnp.float32) + bup_s
    hidden = jax.nn.gelu(pre, approximate=True).astype(jnp.bfloat16)
    partial_value = jnp.dot(hidden, down_s, preferred_element_type=jnp.float32)
    whole = (values + partial_value + bdown_s).astype(jnp.bfloat16)
    return whole.reshape(BATCH, SEQ, D)

def reference(acts, ln_gain, ln_bias, w_up, b_up, w_down, b_down):
    boundary = lax.map(run_section, (acts, ln_gain, ln_bias, w_up, b_up, w_down, b_down))
    return jnp.roll(boundary, 1, axis=0)
```

```python
import functools

import jax
import jax.numpy as jnp
from jax import lax
from jax.experimental import pallas as pl
from jax.experimental.pallas import tpu as pltpu
from jax.sharding import Mesh
from jax.sharding import PartitionSpec as P

BATCH = 2
RING = 4
TILE = 32
PART = 1024
HALF = PART // 2
UNITS = 512
STEP = 256
EPS = 1e-05


def sent(block, axis, distance):
    return lax.ppermute(block, axis, [(i, (i + distance) % RING) for i in range(RING)])


def swapped(block):
    return lax.ppermute(block, "core", [(0, 1), (1, 0)])


def next_section(block, cross):
    pairs = []
    for section in range(8):
        for core in range(2):
            pairs.append((section * 2 + core, (section + 1) % 8 * 2 + (core ^ cross)))
    return lax.ppermute(block, ("y", "zl", "core"), pairs)


def ring_gather(block, axis):
    left = sent(block, axis, 1)
    right = sent(block, axis, -1)
    first = sent(left[..., 0, :, :], axis, 1)
    second = sent(right[..., 1, :, :], axis, -1)
    return left, right, first, second


def feed_forward_kernel(place, *refs):
    own, zs, zz = refs[0:5], refs[5:10], refs[10:15]
    gain, bias, up_o, up_s, b_up, down_o, down_s = refs[15:22]
    outs, resid, normed, total = refs[22:30], refs[30], refs[31], refs[32]
    step = pl.program_id(0)
    x, z = place[0], place[1]

    def piece(j, half, k):
        if k == 0:
            base, lead = own, (0,)
        elif k == 2:
            base, lead = zz, ()
        else:
            base, lead = zs, (0 if k == 3 else 1,)
        if j == 2:
            ref = base[3] if half == 0 else base[4]
            return ref[lead] if lead else ref[...]
        ref = base[{0: 0, 3: 1, 1: 2}[j]]
        return ref[(*lead, half)]

    @pl.when(step == 0)
    def _():
        for j in range(RING):
            for half in range(2):
                row = (x + j) & 3
                seq = row >> 1
                dest = ((row & 1) * 2 + half - x) & 3
                at = pl.multiple_of((dest * 2 + seq) * TILE, TILE)
                raw = [piece(j, half, k) for k in range(RING)]
                values = [r.astype(jnp.float32) for r in raw]
                mean = sum(jnp.sum(v, axis=-1, keepdims=True) for v in values) / (RING * PART)
                centered = [v - mean for v in values]
                spread = sum(jnp.sum(v * v, axis=-1, keepdims=True) for v in centered) / (RING * PART)
                scale = lax.rsqrt(spread + EPS)
                for k in range(RING):
                    true = (z + k) & 3
                    value = centered[k] * scale * gain[pl.ds(true, 1), :] + bias[pl.ds(true, 1), :]
                    normed[true, pl.ds(at, TILE), :] = value.astype(jnp.bfloat16)

                @pl.when(dest == 0)
                def _():
                    resid[seq] = raw[0]

    def work(up, down):
        pre = sum(
            jnp.dot(normed[k], up[pl.ds(k * PART, PART), :], preferred_element_type=jnp.float32)
            for k in range(RING)
        )
        hidden = jax.nn.gelu(pre + b_up[...], approximate=True).astype(jnp.bfloat16)
        for k in range(RING):
            term = jnp.dot(hidden, down[:, pl.ds(k * PART, PART)], preferred_element_type=jnp.float32)

            @pl.when(step == 0)
            def _():
                total[k] = term

            @pl.when(step > 0)
            def _():
                total[k] += term

    @pl.when(step < 2)
    def _():
        work(up_o, down_o)

    @pl.when(step >= 2)
    def _():
        work(up_s, down_s)

    @pl.when(step == 3)
    def _():
        for dest in range(RING):
            for seq in range(2):
                for k in range(RING):
                    true = (z + k) & 3
                    row = (dest * 2 + seq) * TILE
                    outs[dest * 2 + seq][k] = total[true, row : row + TILE, :].astype(jnp.bfloat16)


def feed_forward(part, place, own, zs, zz, gain, bias, up_o, up_s, b_up, down_o, down_s):
    def whole(shape):
        return pl.BlockSpec(shape, lambda g: (0,) * len(shape))

    def half(shape):
        return pl.BlockSpec((1, *shape[1:]), lambda g: (part, *(0,) * (len(shape) - 1)))

    first = lambda g: jnp.minimum(g, 1)
    second = lambda g: jnp.maximum(g - 2, 0)
    wide = RING * PART
    in_specs = (
        [pl.BlockSpec(memory_space=pltpu.SMEM)]
        + [half(a.shape) for a in own]
        + [whole(a.shape) for a in zs]
        + [whole(a.shape) for a in zz]
        + [whole((RING, PART)), whole((RING, PART))]
        + [pl.BlockSpec((wide, STEP), lambda g: (0, first(g)))]
        + [pl.BlockSpec((wide, STEP), lambda g: (0, second(g)))]
        + [pl.BlockSpec((1, STEP), lambda g: (0, g))]
        + [pl.BlockSpec((STEP, wide), lambda g: (first(g), 0))]
        + [pl.BlockSpec((STEP, wide), lambda g: (second(g), 0))]
    )
    piece = jax.ShapeDtypeStruct((RING, TILE, PART), jnp.bfloat16)
    resid = jax.ShapeDtypeStruct((2, TILE, PART), jnp.bfloat16)
    tokens = 2 * RING * TILE
    return pl.pallas_call(
        feed_forward_kernel,
        grid=(4,),
        in_specs=in_specs,
        out_specs=[whole(piece.shape)] * 8 + [whole(resid.shape)],
        out_shape=[piece] * 8 + [resid],
        scratch_shapes=[
            pltpu.VMEM((RING, tokens, PART), jnp.bfloat16),
            pltpu.VMEM((RING, tokens, PART), jnp.float32),
        ],
        compiler_params=pltpu.CompilerParams(
            dimension_semantics=("arbitrary",), vmem_limit_bytes=44 * 1024 * 1024
        ),
        cost_estimate=pl.CostEstimate(
            flops=4 * tokens * wide * 2 * UNITS, bytes_accessed=20 * 1024 * 1024, transcendentals=tokens * 2 * UNITS
        ),
    )(place, *own, *zs, *zz, gain, bias, up_o, up_s, b_up, down_o, down_s)


def added(*terms):
    return sum(t.astype(jnp.float32) for t in terms).astype(jnp.bfloat16)


def shards(acts, ln_gain, ln_bias, w_up, b_up, w_down, b_down):
    x, z, core = (lax.axis_index(a) for a in ("x", "zh", "core"))
    place = jnp.stack([x, z]).astype(jnp.int32)
    up_o, down_o = w_up[0], w_down[0]

    split = acts[0].reshape(2, 2, 2, TILE, HALF)
    mine = lax.dynamic_index_in_dim(split, core, 1, keepdims=False)
    theirs = lax.dynamic_index_in_dim(split, 1 - core, 1, keepdims=False)
    got = swapped(theirs)
    b_up_s = swapped(b_up)
    up_s, down_s = swapped(up_o), swapped(down_o)
    low = jnp.where(core == 0, mine, got)
    high = jnp.where(core == 0, got, mine)
    block = jnp.concatenate([low, high], axis=-1).transpose(1, 0, 2, 3)

    gain, bias = ln_gain[0].reshape(RING, PART), ln_bias[0].reshape(RING, PART)
    b_all = jnp.concatenate([b_up, b_up_s], axis=1)
    own = (block, *ring_gather(block, "x"))

    results = []
    for part in range(2):
        left, right, first, second = ring_gather(block[part], "zh")
        zs = jnp.stack([left, right])
        zz = jnp.stack([first, second])
        zs = (zs, *ring_gather(zs, "x"))
        zz = (zz, *ring_gather(zz, "x"))
        *out, resid = feed_forward(part, place, own, zs, zz, gain, bias, up_o, up_s, b_all, down_o, down_s)
        out = [out[2 * k : 2 * k + 2] for k in range(RING)]
        far_l = sent(out[2][0], "x", 1)
        far_r = sent(out[2][1], "x", -1)
        from_l1 = sent(out[1][1], "x", 1)
        from_r0 = sent(out[3][0], "x", -1)
        from_l0 = sent(added(out[1][0], far_l), "x", 1)
        from_r1 = sent(added(out[3][1], far_r), "x", -1)
        s0 = added(out[0][0], from_l0, from_r0)
        s1 = added(out[0][1], from_l1, from_r1)
        far_l = sent(s0[2], "zh", 1)
        far_r = sent(s1[2], "zh", -1)
        from_l = sent(jnp.stack([added(s0[1], far_l), s1[1]]), "zh", 1)
        from_r = sent(jnp.stack([s0[3], added(s1[3], far_r)]), "zh", -1)
        shift = lax.dynamic_slice_in_dim(b_down[0], z * PART, PART, 0)
        value = (
            jnp.stack([s0[0], s1[0]]).astype(jnp.float32)
            + from_l.astype(jnp.float32)
            + from_r.astype(jnp.float32)
            + resid.astype(jnp.float32)
            + shift
        ).astype(jnp.bfloat16)
        low, high = value[..., :HALF], value[..., HALF:]
        keep = next_section(jnp.where(core == 0, low, high), 0)
        cross = next_section(jnp.where(core == 0, high, low), 1)
        results.append(jnp.stack([jnp.where(core == 0, keep, cross), jnp.where(core == 0, cross, keep)], axis=1))
    out = jnp.stack(results, axis=2)
    return out.reshape(1, BATCH, 4 * TILE, HALF)


def solution(mesh):
    fine = Mesh(mesh.devices.reshape(4, 2, 4, 4, 2), ("y", "zl", "x", "zh", "core"))
    section, rows, hid = ("y", "zl"), "x", ("zh", "core")
    in_specs = (
        P(section, rows, hid),
        P(section, None),
        P(section, None),
        P(section, None, ("x", "zh", "core")),
        P(section, ("x", "zh", "core")),
        P(section, ("x", "zh", "core"), None),
        P(section, None),
    )
    out_specs = P(section, None, rows, hid)
    return jax.shard_map(shards, mesh=fine, in_specs=in_specs, out_specs=out_specs, check_vma=False)
```

```python
import jax
import jax.numpy as jnp
from jax import lax
from jax.experimental import pallas as pl
from jax.experimental.pallas import tpu as pltpu
from jax.sharding import Mesh
from jax.sharding import PartitionSpec as P

BATCH = 2
RING = 4
TILE = 64
PART = 1024
HALF = PART // 2
UNITS = 512
STEP = 256
ROWS = 16
UNROLL = 4
EPS = 1e-05
MIB = 1024 * 1024
LIMIT = 16
COST = 4
BYTES = MIB


def sent(block, axis, distance):
    return lax.ppermute(block, axis, [(i, (i + distance) % RING) for i in range(RING)])


def swapped(block):
    return lax.ppermute(block, "core", [(0, 1), (1, 0)])


def next_section(block, cross):
    pairs = []
    for section in range(8):
        for core in range(2):
            pairs.append((section * 2 + core, (section + 1) % 8 * 2 + (core ^ cross)))
    return lax.ppermute(block, ("y", "zl", "core"), pairs)


def added(*terms):
    return sum(t.astype(jnp.float32) for t in terms).astype(jnp.bfloat16)


def normalize(pieces, z, gain, bias, normed, at, rows):
    def some(i, _):
        start = pl.multiple_of(i * ROWS, ROWS)
        values = [read(start).astype(jnp.float32) for read in pieces]
        mean = sum(jnp.sum(v, axis=-1, keepdims=True) for v in values) / (RING * PART)
        centered = [v - mean for v in values]
        spread = sum(jnp.sum(v * v, axis=-1, keepdims=True) for v in centered) / (RING * PART)
        scale = lax.rsqrt(spread + EPS)
        for k in range(RING):
            true = (z + k) & 3
            value = centered[k] * scale * gain[pl.ds(true, 1), :] + bias[pl.ds(true, 1), :]
            normed[true, pl.ds(at + start, ROWS), :] = value.astype(jnp.bfloat16)
        return 0

    lax.fori_loop(0, rows // ROWS, some, 0, unroll=UNROLL)


def reader(ref, *lead):
    return lambda start: ref[(*lead, pl.ds(start, ROWS), slice(None))]


def halves(ref, *lead, first=0):
    return lambda start: ref[(*lead, first + start // TILE, pl.ds(pl.multiple_of(start % TILE, ROWS), ROWS), slice(None))]


def up(normed, ups, b_up, store):
    def some(n, _):
        columns = pl.ds(pl.multiple_of((n & 1) * STEP, STEP), STEP)
        pre = b_up[pl.ds(n >> 1, 1), columns]
        for k in range(RING):
            pre = pre + jnp.dot(
                normed[k], ups[n >> 1, pl.ds(k * PART, PART), columns], preferred_element_type=jnp.float32
            )
        store(pl.ds(pl.multiple_of(n * STEP, STEP), STEP), jax.nn.gelu(pre, approximate=True).astype(jnp.bfloat16))
        return 0

    lax.fori_loop(0, 2 * UNITS // STEP, some, 0)


def near_kernel(place, block, zs, zz, xm, sm, mr, xp, sp, ml, gain, bias, b_up, ups, hidden, normed):
    z = place[1]
    for slot, (a, b, c) in enumerate(((block, zs, zz), (xm, sm, mr), (xp, sp, ml))):
        pieces = [halves(a), halves(b, 1), halves(c, first=2 if slot else 0), halves(b, 0)]
        normalize(pieces, z, gain, bias, normed, slot * 2 * TILE, 2 * TILE)

    def store(columns, value):
        for tile in range(6):
            hidden[tile, :, columns] = value[tile * TILE : (tile + 1) * TILE]

    up(normed, ups, b_up, store)


def down(z, hid, downs, offset, stride, group, outs):
    plus, minus, left, right, own = outs
    homes = {
        (0, 0): (own, (0,)), (0, 1): (own, (1,)), (1, 0): (left, ()), (1, 1): (plus, (1,)),
        (2, 0): (plus, (0,)), (2, 1): (minus, (0,)), (3, 0): (minus, (1,)), (3, 1): (right, ()),
    }

    def some(i, _):
        n, t = i >> 1, i & 1
        columns = pl.ds(pl.multiple_of(t * HALF, HALF), HALF)
        start = pl.ds(pl.multiple_of(((z + offset + stride * n) & 3) * PART + t * HALF, HALF), HALF)
        rows = hid[...].reshape(8 * TILE, 2 * UNITS)
        term = jnp.dot(rows[:, :UNITS], downs[0, :, start], preferred_element_type=jnp.float32)
        term = term + jnp.dot(rows[:, UNITS:], downs[1, :, start], preferred_element_type=jnp.float32)
        term = term.astype(jnp.bfloat16)
        for (dest, seq), (ref, lead) in homes.items():
            at = (dest * 2 + seq) * TILE
            ref[(*lead, n, slice(None), columns)] = term[at : at + TILE]
        return 0

    lax.fori_loop(0, group * PART // HALF, some, 0)


def far_kernel(place, ml, mr, nl, nr, gain, bias, b_up, near, ups, downs,
               plus, minus, left, right, own, hid, normed):
    x, z = place[0], place[1]

    def home(j, half):
        row = (x + j) & 3
        return (((row & 1) * 2 + half - x) & 3) * 2 + (row >> 1)

    for half, (a, b) in enumerate(((ml, nl), (mr, nr))):
        pieces = [reader(b, 1), reader(a, 1), reader(b, 0), reader(a, 0)]
        normalize(pieces, z, gain, bias, normed, half * TILE, TILE)
    for slot, j in enumerate((0, 1, 3)):
        for half in range(2):
            hid[home(j, half)] = near[slot * 2 + half]

    def store(columns, value):
        for half in range(2):
            hid[home(2, half), :, columns] = value[half * TILE : (half + 1) * TILE]

    up(normed, ups, b_up, store)
    down(z, hid, downs, 2, 0, 1, (plus, minus, left, right, own))


def side_kernel(place, hid, downs, plus, minus, left, right, own):
    down(place[1], hid, downs, 1, 2, 2, (plus, minus, left, right, own))


def own_kernel(place, hid, downs, block, xm, nl, nr, xp, plus, minus, left, right, own, resid):
    x = place[0]
    for seq in range(2):
        row, half = 2 * seq + (x >> 1), x & 1
        j = (row - x) & 3
        for at, ref in ((0, block), (1, xm), (3, xp)):

            @pl.when(j == at)
            def _(ref=ref):
                resid[seq] = ref[half]

        @pl.when((j == 2) & (half == 0))
        def _():
            resid[seq] = nl[1]

        @pl.when((j == 2) & (half == 1))
        def _():
            resid[seq] = nr[1]

    down(place[1], hid, downs, 0, 0, 1, (plus, minus, left, right, own))


VMEM = pl.BlockSpec(memory_space=pltpu.VMEM)
SMEM = pl.BlockSpec(memory_space=pltpu.SMEM)


def call(kernel, out_shape, scratch, flops, *operands):
    return pl.pallas_call(
        kernel,
        in_specs=[SMEM] + [VMEM] * (len(operands) - 1),
        out_specs=[VMEM] * len(out_shape),
        out_shape=out_shape,
        scratch_shapes=scratch,
        compiler_params=pltpu.CompilerParams(vmem_limit_bytes=LIMIT * MIB),
        cost_estimate=pl.CostEstimate(flops=flops // COST, bytes_accessed=BYTES, transcendentals=0),
    )(*operands)


def group_shapes(group):
    two = jax.ShapeDtypeStruct((2, group, TILE, PART), jnp.bfloat16)
    one = jax.ShapeDtypeStruct((group, TILE, PART), jnp.bfloat16)
    return [two, two, one, one, two]


def load_kernel(own, other, out, token, sems):
    copies = [pltpu.make_async_copy(ref, out.at[i], sems.at[i]) for i, ref in enumerate((own, other))]
    for copy in copies:
        copy.start()
    token[...] = jnp.zeros_like(token)
    for copy in copies:
        copy.wait()


def loaded(own, other):
    return pl.pallas_call(
        load_kernel,
        in_specs=[pl.BlockSpec(memory_space=pltpu.HBM)] * 2,
        out_specs=[VMEM, VMEM],
        out_shape=[pltpu.VMEM((2, *own.shape), own.dtype), jax.ShapeDtypeStruct((8, 128), jnp.float32)],
        scratch_shapes=[pltpu.SemaphoreType.DMA((2,))],
        compiler_params=pltpu.CompilerParams(vmem_limit_bytes=LIMIT * MIB),
        cost_estimate=pl.CostEstimate(flops=0, bytes_accessed=16 * MIB, transcendentals=0),
    )(own, other)


def compute(place, block, zs, zz, xm, sm, mr, xp, sp, ml, nl, nr,
            gain, bias, b_all, ups, downs):
    mul = 2 * 2 * UNITS * RING * PART
    near = call(
        near_kernel,
        [jax.ShapeDtypeStruct((6, TILE, 2 * UNITS), jnp.bfloat16)],
        [pltpu.VMEM((RING, 6 * TILE, PART), jnp.bfloat16)],
        6 * TILE * mul,
        place, block, zs, zz, xm, sm, mr, xp, sp, ml, gain, bias, b_all, ups,
    )[0]
    *two, hid = call(
        far_kernel,
        group_shapes(1) + [jax.ShapeDtypeStruct((8, TILE, 2 * UNITS), jnp.bfloat16)],
        [pltpu.VMEM((RING, 2 * TILE, PART), jnp.bfloat16)],
        2 * TILE * mul + 2 * TILE * mul,
        place, ml, mr, nl, nr, gain, bias, b_all, near, ups, downs,
    )
    side = call(
        side_kernel, group_shapes(2), [], 4 * TILE * mul,
        place, hid, downs,
    )
    return two, side, hid


def shards(acts, ln_gain, ln_bias, w_up, b_up, w_down, b_down):
    x, z, core = (lax.axis_index(a) for a in ("x", "zh", "core"))
    place = jnp.stack([x, z]).astype(jnp.int32)
    up_o, down_o = w_up[0], w_down[0]
    gain, bias = ln_gain[0].reshape(RING, PART), ln_bias[0].reshape(RING, PART)

    split = acts[0].reshape(2, 2, TILE, HALF)
    mine = lax.dynamic_index_in_dim(split, core, 1, keepdims=False)
    theirs = lax.dynamic_index_in_dim(split, 1 - core, 1, keepdims=False)
    got, b_up_s = lax.optimization_barrier((swapped(theirs), swapped(b_up)))
    low = jnp.where(core == 0, mine, got)
    high = jnp.where(core == 0, got, mine)
    block = jnp.concatenate([low, high], axis=-1)
    block, up_o = lax.optimization_barrier((block, up_o))
    b_all = jnp.concatenate([b_up, b_up_s], axis=0)

    zp, zm = sent(block, "zh", 1), sent(block, "zh", -1)
    xp, xm = sent(block, "x", 1), sent(block, "x", -1)
    up_s = swapped(up_o)
    zp, zm, xp, xm, up_s, down_o = lax.optimization_barrier((zp, zm, xp, xm, up_s, down_o))
    zs = jnp.stack([zp, zm])
    za, zb = sent(zp[0], "zh", 1), sent(zm[1], "zh", -1)
    sp, sm = sent(zs, "x", 1), sent(zs, "x", -1)
    down_s = swapped(down_o)
    ups, token = loaded(up_o, up_s)
    za, zb, sp, sm, xp, xm, token = lax.optimization_barrier((za, zb, sp, sm, xp, xm, token))
    place = place + token[0, :2].astype(jnp.int32)
    zz = jnp.stack([za, zb])
    ml = sent(jnp.concatenate([sp[:, 0], zz]), "x", 1)
    mr = sent(jnp.concatenate([sm[:, 1], zz]), "x", -1)
    downs, token = loaded(down_o, down_s)
    ml, mr, xp, xm, token = lax.optimization_barrier((ml, mr, xp, xm, token))
    place = place + token[0, :2].astype(jnp.int32)
    nl = sent(jnp.stack([ml[2], xp[0]]), "x", 1)
    nr = sent(jnp.stack([mr[3], xm[1]]), "x", -1)

    two, side, hid = compute(place, block, zs, zz, xm, sm, mr, xp, sp, ml, nl, nr,
                             gain, bias, b_all, ups, downs)

    def first_step(plus, minus, *_):
        return lax.optimization_barrier((sent(plus, "x", 1), sent(minus, "x", -1)))

    def second_step(parts, l, r):
        return lax.optimization_barrier((sent(added(parts[2], l[0]), "x", 1), sent(added(parts[3], r[0]), "x", -1)))

    def summed(parts, l, r, fl, fr):
        own = parts[4]
        return added(own[0], fl, r[1]), added(own[1], l[1], fr)

    l2, r2 = first_step(*two)
    l2, r2, hid = lax.optimization_barrier((l2, r2, hid))
    *last, resid = call(
        own_kernel, group_shapes(1) + [jax.ShapeDtypeStruct((2, TILE, PART), jnp.bfloat16)], [], 2 * TILE * 2 * 2 * UNITS * RING * PART,
        place, hid, downs, block, xm, nl, nr, xp,
    )
    fl2, fr2 = second_step(two, l2, r2)
    l1, r1 = first_step(*side)
    s0, s1 = summed(two, l2, r2, fl2, fr2)
    zl, zr = lax.optimization_barrier((sent(s0, "zh", 1), sent(s1, "zh", -1)))
    plus, minus, l1, r1 = lax.optimization_barrier((*last[:2], l1, r1))
    fl1, fr1 = second_step(side, l1, r1)
    l0, r0 = first_step(plus, minus)
    t0, t1 = summed(side, l1, r1, fl1, fr1)
    zfl = sent(jnp.stack([added(t0[:1], zl), t1[:1]]), "zh", 1)
    zfr = sent(jnp.stack([t0[1:], added(t1[1:], zr)]), "zh", -1)
    fl0, fr0 = second_step(last, l0, r0)
    shift = lax.dynamic_slice_in_dim(b_down[0], z * PART, PART, 0)
    own = last[4]
    value = jnp.concatenate(
        [
            added(own[0], fl0, r0[1], zfl[0], zfr[0], resid[:1], shift),
            added(own[1], l0[1], fr0, zfl[1], zfr[1], resid[1:], shift),
        ]
    )
    low, high = value[..., :HALF], value[..., HALF:]
    keep = next_section(jnp.where(core == 0, low, high), 0)
    cross = next_section(jnp.where(core == 0, high, low), 1)
    out = jnp.stack([jnp.where(core == 0, keep, cross), jnp.where(core == 0, cross, keep)], axis=1)
    return out.reshape(1, BATCH, 2 * TILE, HALF)


def solution(mesh):
    fine = Mesh(mesh.devices.reshape(4, 2, 4, 4, 2), ("y", "zl", "x", "zh", "core"))
    section, rows, hid = ("y", "zl"), "x", ("zh", "core")
    in_specs = (
        P(section, rows, hid),
        P(section, None),
        P(section, None),
        P(section, None, ("x", "zh", "core")),
        P(section, ("x", "zh", "core")),
        P(section, ("x", "zh", "core"), None),
        P(section, None),
    )
    out_specs = P(section, None, rows, hid)
    return jax.shard_map(shards, mesh=fine, in_specs=in_specs, out_specs=out_specs, check_vma=False)
```

```python
import jax
import jax.numpy as jnp
from jax import lax
from jax.experimental import pallas as pl
from jax.experimental.pallas import tpu as pltpu
from jax.sharding import Mesh
from jax.sharding import PartitionSpec as P

BATCH = 2
RING = 4
TILE = 64
PART = 1024
HALF = PART // 2
UNITS = 512
STEP = 256
ROWS = 16
UNROLL = 4
EPS = 1e-05
MIB = 1024 * 1024
LIMIT = 8
COST = 4
BYTES = MIB


def sent(block, axis, distance):
    return lax.ppermute(block, axis, [(i, (i + distance) % RING) for i in range(RING)])


def swapped(block):
    return lax.ppermute(block, "core", [(0, 1), (1, 0)])


def next_section(block, cross):
    pairs = []
    for section in range(8):
        for core in range(2):
            pairs.append((section * 2 + core, (section + 1) % 8 * 2 + (core ^ cross)))
    return lax.ppermute(block, ("y", "zl", "core"), pairs)


def added(*terms):
    return sum(t.astype(jnp.float32) for t in terms).astype(jnp.bfloat16)


def normalize(pieces, z, gain, bias, normed, at, rows):
    def some(i, _):
        start = pl.multiple_of(i * ROWS, ROWS)
        values = [read(start).astype(jnp.float32) for read in pieces]
        mean = sum(jnp.sum(v, axis=-1, keepdims=True) for v in values) / (RING * PART)
        centered = [v - mean for v in values]
        spread = sum(jnp.sum(v * v, axis=-1, keepdims=True) for v in centered) / (RING * PART)
        scale = lax.rsqrt(spread + EPS)
        for k in range(RING):
            true = (z + k) & 3
            value = centered[k] * scale * gain[pl.ds(true, 1), :] + bias[pl.ds(true, 1), :]
            normed[true, pl.ds(at + start, ROWS), :] = value.astype(jnp.bfloat16)
        return 0

    lax.fori_loop(0, rows // ROWS, some, 0, unroll=UNROLL)


def reader(ref, *lead):
    return lambda start: ref[(*lead, pl.ds(start, ROWS), slice(None))]


def halves(ref, *lead):
    return lambda start: ref[(*lead, start // TILE, pl.ds(pl.multiple_of(start % TILE, ROWS), ROWS), slice(None))]


def up(normed, ups, b_up, store):
    def some(n, _):
        columns = pl.ds(pl.multiple_of((n & 1) * STEP, STEP), STEP)
        pre = b_up[pl.ds(n >> 1, 1), columns]
        for k in range(RING):
            pre = pre + jnp.dot(
                normed[k], ups[n >> 1, pl.ds(k * PART, PART), columns], preferred_element_type=jnp.float32
            )
        store(pl.ds(pl.multiple_of(n * STEP, STEP), STEP), jax.nn.gelu(pre, approximate=True).astype(jnp.bfloat16))
        return 0

    lax.fori_loop(0, 2 * UNITS // STEP, some, 0)


def near_kernel(place, block, zs, zz, xm, sm, qm, xp, sp, qp, gain, bias, b_up, ups, hidden, normed):
    z = place[1]
    for slot, (a, b, c) in enumerate(((block, zs, zz), (xm, sm, qm), (xp, sp, qp))):
        pieces = [halves(a), halves(b, 1), halves(c), halves(b, 0)]
        normalize(pieces, z, gain, bias, normed, slot * 2 * TILE, 2 * TILE)

    def store(columns, value):
        for tile in range(6):
            hidden[tile, :, columns] = value[tile * TILE : (tile + 1) * TILE]

    up(normed, ups, b_up, store)


def down(z, rows, downs, store):
    def some(i, _):
        n, t = i >> 1, i & 1
        k = jnp.where(n == 0, 2, jnp.where(n == 3, 0, 2 * n - 1))
        start = pl.ds(pl.multiple_of(((z + k) & 3) * PART + t * HALF, HALF), HALF)
        value = rows()
        term = jnp.dot(value[:, :UNITS], downs[0, :, start], preferred_element_type=jnp.float32)
        term = term + jnp.dot(value[:, UNITS:], downs[1, :, start], preferred_element_type=jnp.float32)
        store(n, pl.ds(pl.multiple_of(t * HALF, HALF), HALF), term.astype(jnp.bfloat16))
        return 0

    lax.fori_loop(0, RING * PART // HALF, some, 0)


def far_kernel(place, ml, mr, gain, bias, b_up, near, ups, downs, plus, minus, hid, normed):
    x, z = place[0], place[1]

    def home(j, half):
        row = (x + j) & 3
        dest = ((row & 1) * 2 + half - x) & 3
        return (dest ^ (dest >> 1)) * 2 + (row >> 1)

    for half, a in enumerate((ml, mr)):
        pieces = [reader(a, 3), reader(a, 1), reader(a, 2), reader(a, 0)]
        normalize(pieces, z, gain, bias, normed, half * TILE, TILE)
    for slot, j in enumerate((0, 1, 3)):
        for half in range(2):
            hid[home(j, half)] = near[slot * 2 + half]

    def store(columns, value):
        for half in range(2):
            hid[home(2, half), :, columns] = value[half * TILE : (half + 1) * TILE]

    up(normed, ups, b_up, store)

    def send(n, columns, value):
        plus[n, :, columns] = value[:TILE]
        minus[n, :, columns] = value[TILE:]

    down(z, lambda: hid[6:8].reshape(2 * TILE, 2 * UNITS), downs, send)


def rest_kernel(place, hid, downs, block, xm, ml, mr, xp, own, plus, minus, resid):
    x, z = place[0], place[1]
    for seq in range(2):
        row, half = 2 * seq + (x >> 1), x & 1
        j = (row - x) & 3
        for at, ref in ((0, block), (1, xm), (3, xp)):

            @pl.when(j == at)
            def _(ref=ref):
                resid[seq] = ref[half]

        @pl.when((j == 2) & (half == 0))
        def _():
            resid[seq] = ml[3]

        @pl.when((j == 2) & (half == 1))
        def _():
            resid[seq] = mr[3]

    def store(n, columns, value):
        for k, ref in enumerate((own, plus, minus)):
            for seq in range(2):
                at = (k * 2 + seq) * TILE
                ref[seq, n, :, columns] = value[at : at + TILE]

    down(z, lambda: hid[0:6].reshape(6 * TILE, 2 * UNITS), downs, store)


VMEM = pl.BlockSpec(memory_space=pltpu.VMEM)
SMEM = pl.BlockSpec(memory_space=pltpu.SMEM)


def call(kernel, out_shape, scratch, flops, *operands):
    return pl.pallas_call(
        kernel,
        in_specs=[SMEM] + [VMEM] * (len(operands) - 1),
        out_specs=[VMEM] * len(out_shape),
        out_shape=out_shape,
        scratch_shapes=scratch,
        compiler_params=pltpu.CompilerParams(vmem_limit_bytes=LIMIT * MIB),
        cost_estimate=pl.CostEstimate(flops=flops // COST, bytes_accessed=BYTES, transcendentals=0),
    )(*operands)


def load_kernel(own, other, after, out, token, sems):
    del after
    copies = [pltpu.make_async_copy(ref, out.at[i], sems.at[i]) for i, ref in enumerate((own, other))]
    for copy in copies:
        copy.start()
    token[...] = jnp.zeros_like(token)
    for copy in copies:
        copy.wait()


def loaded(own, other, after):
    return pl.pallas_call(
        load_kernel,
        in_specs=[pl.BlockSpec(memory_space=pltpu.HBM)] * 2 + [pl.BlockSpec(memory_space=pl.ANY)],
        out_specs=[VMEM, VMEM],
        out_shape=[pltpu.VMEM((2, *own.shape), own.dtype), jax.ShapeDtypeStruct((8, 128), jnp.float32)],
        scratch_shapes=[pltpu.SemaphoreType.DMA((2,))],
        compiler_params=pltpu.CompilerParams(vmem_limit_bytes=LIMIT * MIB),
        cost_estimate=pl.CostEstimate(flops=0, bytes_accessed=16 * MIB, transcendentals=0),
    )(own, other, after)


def compute(place, far_place, near, block, xm, xp, ml, mr, gain, bias, b_all, ups, downs):
    mul = 2 * 2 * UNITS * RING * PART
    far = call(
        far_kernel,
        [jax.ShapeDtypeStruct((RING, TILE, PART), jnp.bfloat16)] * 2
        + [jax.ShapeDtypeStruct((8, TILE, 2 * UNITS), jnp.bfloat16)],
        [pltpu.VMEM((RING, 2 * TILE, PART), jnp.bfloat16)],
        4 * TILE * mul,
        far_place, ml, mr, gain, bias, b_all, near, ups, downs,
    )
    rest = call(
        rest_kernel,
        [jax.ShapeDtypeStruct((2, RING, TILE, PART), jnp.bfloat16)] * 3
        + [jax.ShapeDtypeStruct((2, TILE, PART), jnp.bfloat16)],
        [],
        6 * TILE * mul,
        place, far[2], downs, block, xm, ml, mr, xp,
    )
    return far[:2], rest


def shards(acts, ln_gain, ln_bias, w_up, b_up, w_down, b_down):
    x, z, core = (lax.axis_index(a) for a in ("x", "zh", "core"))
    place = jnp.stack([x, z]).astype(jnp.int32)
    up_o, down_o = w_up[0], w_down[0]
    gain, bias = ln_gain[0].reshape(RING, PART), ln_bias[0].reshape(RING, PART)

    split = acts[0].reshape(2, 2, TILE, HALF)
    mine = lax.dynamic_index_in_dim(split, core, 1, keepdims=False)
    theirs = lax.dynamic_index_in_dim(split, 1 - core, 1, keepdims=False)
    got, b_up_s = lax.optimization_barrier((swapped(theirs), swapped(b_up)))
    low = jnp.where(core == 0, mine, got)
    high = jnp.where(core == 0, got, mine)
    block = jnp.concatenate([low, high], axis=-1)
    block, up_o = lax.optimization_barrier((block, up_o))
    b_all = jnp.concatenate([b_up, b_up_s], axis=0)

    zp, zm = sent(block, "zh", 1), sent(block, "zh", -1)
    xp, xm = sent(block, "x", 1), sent(block, "x", -1)
    up_s = swapped(up_o)
    zp, zm, xp, xm, up_s, down_o = lax.optimization_barrier((zp, zm, xp, xm, up_s, down_o))
    zs = jnp.stack([zp, zm])
    sp, sm = sent(zs, "x", 1), sent(zs, "x", -1)
    za, zb = sent(zp[0], "zh", 1), sent(zm[1], "zh", -1)
    za, zb = lax.optimization_barrier((za, zb))
    zz = jnp.stack([za, zb])
    qp, qm = sent(zz, "x", 1), sent(zz, "x", -1)
    down_s = swapped(down_o)
    ups, token = loaded(up_o, up_s, b_all)
    sp, sm, qp, qm, xp, xm, token = lax.optimization_barrier((sp, sm, qp, qm, xp, xm, token))
    place = place + token[0, :2].astype(jnp.int32)
    ml = sent(jnp.stack([sp[0, 0], sp[1, 0], qp[0], xp[0]]), "x", 1)
    mr = sent(jnp.stack([sm[0, 1], sm[1, 1], qm[1], xm[1]]), "x", -1)
    near = call(
        near_kernel,
        [jax.ShapeDtypeStruct((6, TILE, 2 * UNITS), jnp.bfloat16)],
        [pltpu.VMEM((RING, 6 * TILE, PART), jnp.bfloat16)],
        6 * TILE * 4 * UNITS * RING * PART,
        place, block, zs, zz, xm, sm, qm, xp, sp, qp, gain, bias, b_all, ups,
    )[0]
    downs, token = loaded(down_o, down_s, near)
    far_place = place + token[0, :2].astype(jnp.int32)

    (far_l, far_r), (own, plus, minus, resid) = compute(
        place, far_place, near, block, xm, xp, ml, mr, gain, bias, b_all, ups, downs
    )
    l, r = lax.optimization_barrier((sent(far_l, "x", 1), sent(far_r, "x", -1)))

    def over_x(first, last):
        to_left = jnp.stack([added(plus[0, first:last], l[first:last]), plus[1, first:last]])
        to_right = jnp.stack([minus[0, first:last], added(minus[1, first:last], r[first:last])])
        return lax.optimization_barrier((sent(to_left, "x", 1), sent(to_right, "x", -1)))

    fl2, fr2 = over_x(0, 1)
    fl1, fr1 = over_x(1, 3)
    fl0, fr0 = over_x(3, 4)
    s2 = added(own[:, 0], fl2[:, 0], fr2[:, 0])
    zl, zr = lax.optimization_barrier((sent(s2[0], "zh", 1), sent(s2[1], "zh", -1)))
    t = added(own[:, 1:3], fl1, fr1)
    zfl = sent(jnp.stack([added(t[0, 0], zl), t[1, 0]]), "zh", 1)
    zfr = sent(jnp.stack([t[0, 1], added(t[1, 1], zr)]), "zh", -1)
    zfl, zfr, fl0, fr0 = lax.optimization_barrier((zfl, zfr, fl0, fr0))
    shift = lax.dynamic_slice_in_dim(b_down[0], z * PART, PART, 0)
    value = added(own[:, 3], fl0[:, 0], fr0[:, 0], zfl, zfr, resid, shift)
    low, high = value[..., :HALF], value[..., HALF:]
    keep = next_section(jnp.where(core == 0, low, high), 0)
    cross = next_section(jnp.where(core == 0, high, low), 1)
    out = jnp.stack([jnp.where(core == 0, keep, cross), jnp.where(core == 0, cross, keep)], axis=1)
    return out.reshape(1, BATCH, 2 * TILE, HALF)


def solution(mesh):
    fine = Mesh(mesh.devices.reshape(4, 2, 4, 4, 2), ("y", "zl", "x", "zh", "core"))
    section, rows, hid = ("y", "zl"), "x", ("zh", "core")
    in_specs = (
        P(section, rows, hid),
        P(section, None),
        P(section, None),
        P(section, None, ("x", "zh", "core")),
        P(section, ("x", "zh", "core")),
        P(section, ("x", "zh", "core"), None),
        P(section, None),
    )
    out_specs = P(section, None, rows, hid)
    return jax.shard_map(shards, mesh=fine, in_specs=in_specs, out_specs=out_specs, check_vma=False)
```

```python
import jax
import jax.numpy as jnp
from jax import lax
from jax.experimental import pallas as pl
from jax.experimental.pallas import tpu as pltpu
from jax.sharding import Mesh
from jax.sharding import PartitionSpec as P

BATCH = 2
RING = 4
TILE = 64
PART = 1024
HALF = PART // 2
UNITS = 512
STEP = 256
ROWS = 16
UNROLL = 4
EPS = 1e-05
MIB = 1024 * 1024
LIMIT = 8
COST = 4
BYTES = MIB


def sent(block, axis, distance):
    return lax.ppermute(block, axis, [(i, (i + distance) % RING) for i in range(RING)])


def swapped(block):
    return lax.ppermute(block, "core", [(0, 1), (1, 0)])


def next_section(block, cross):
    pairs = []
    for section in range(8):
        for core in range(2):
            pairs.append((section * 2 + core, (section + 1) % 8 * 2 + (core ^ cross)))
    return lax.ppermute(block, ("y", "zl", "core"), pairs)


def added(*terms):
    return sum(t.astype(jnp.float32) for t in terms).astype(jnp.bfloat16)


def normalize(pieces, z, gain, bias, normed, at, rows):
    def some(i, _):
        start = pl.multiple_of(i * ROWS, ROWS)
        values = [read(start).astype(jnp.float32) for read in pieces]
        mean = sum(jnp.sum(v, axis=-1, keepdims=True) for v in values) / (RING * PART)
        centered = [v - mean for v in values]
        spread = sum(jnp.sum(v * v, axis=-1, keepdims=True) for v in centered) / (RING * PART)
        scale = lax.rsqrt(spread + EPS)
        for k in range(RING):
            true = (z + k) & 3
            value = centered[k] * scale * gain[pl.ds(true, 1), :] + bias[pl.ds(true, 1), :]
            normed[true, pl.ds(at + start, ROWS), :] = value.astype(jnp.bfloat16)
        return 0

    lax.fori_loop(0, rows // ROWS, some, 0, unroll=UNROLL)


def reader(ref, *lead):
    return lambda start: ref[(*lead, pl.ds(start, ROWS), slice(None))]


def halves(ref, *lead):
    return lambda start: ref[(*lead, start // TILE, pl.ds(pl.multiple_of(start % TILE, ROWS), ROWS), slice(None))]


def up(normed, ups, b_up, store, unroll=1):
    def some(n, _):
        columns = pl.ds(pl.multiple_of((n & 1) * STEP, STEP), STEP)
        pre = b_up[pl.ds(n >> 1, 1), columns]
        for k in range(RING):
            pre = pre + jnp.dot(
                normed[k], ups[n >> 1, pl.ds(k * PART, PART), columns], preferred_element_type=jnp.float32
            )
        store(pl.ds(pl.multiple_of(n * STEP, STEP), STEP), jax.nn.gelu(pre, approximate=True).astype(jnp.bfloat16))
        return 0

    lax.fori_loop(0, 2 * UNITS // STEP, some, 0, unroll=unroll)


def near_kernel(place, block, zs, zz, xm, sm, qm, xp, sp, qp, gain, bias, b_up, ups, hidden, normed):
    z = place[1]
    for slot, (a, b, c) in enumerate(((block, zs, zz), (xm, sm, qm), (xp, sp, qp))):
        pieces = [halves(a), halves(b, 1), halves(c), halves(b, 0)]
        normalize(pieces, z, gain, bias, normed, slot * 2 * TILE, 2 * TILE)

    def store(columns, value):
        for tile in range(6):
            hidden[tile, :, columns] = value[tile * TILE : (tile + 1) * TILE]

    up(normed, ups, b_up, store)


def down(z, rows, downs, store, wide=HALF, unroll=1):
    each = PART // wide

    def some(i, _):
        n, t = i // each, i % each
        k = jnp.where(n == 0, 2, jnp.where(n == 3, 0, 2 * n - 1))
        start = pl.ds(pl.multiple_of(((z + k) & 3) * PART + t * wide, wide), wide)
        value = rows()
        term = jnp.dot(value[:, :UNITS], downs[0, :, start], preferred_element_type=jnp.float32)
        term = term + jnp.dot(value[:, UNITS:], downs[1, :, start], preferred_element_type=jnp.float32)
        store(n, pl.ds(pl.multiple_of(t * wide, wide), wide), term.astype(jnp.bfloat16))
        return 0

    lax.fori_loop(0, RING * each, some, 0, unroll=unroll)


def far_kernel(place, ml, mr, gain, bias, b_up, near, ups, downs, plus, minus, hid, normed):
    x, z = place[0], place[1]

    def home(j, half):
        row = (x + j) & 3
        dest = ((row & 1) * 2 + half - x) & 3
        return (dest ^ (dest >> 1)) * 2 + (row >> 1)

    for half, a in enumerate((ml, mr)):
        pieces = [reader(a, 3), reader(a, 1), reader(a, 2), reader(a, 0)]
        normalize(pieces, z, gain, bias, normed, half * TILE, TILE)
    for slot, j in enumerate((0, 1, 3)):
        for half in range(2):
            hid[home(j, half)] = near[slot * 2 + half]

    def store(columns, value):
        for half in range(2):
            hid[home(2, half), :, columns] = value[half * TILE : (half + 1) * TILE]

    up(normed, ups, b_up, store, unroll=4)

    def send(n, columns, value):
        plus[n, :, columns] = value[:TILE]
        minus[n, :, columns] = value[TILE:]

    down(z, lambda: hid[6:8].reshape(2 * TILE, 2 * UNITS), downs, send, unroll=4)


def rest_kernel(place, hid, downs, block, xm, ml, mr, xp, own, plus, minus, resid):
    x, z = place[0], place[1]
    for seq in range(2):
        row, half = 2 * seq + (x >> 1), x & 1
        j = (row - x) & 3
        for at, ref in ((0, block), (1, xm), (3, xp)):

            @pl.when(j == at)
            def _(ref=ref):
                resid[seq] = ref[half]

        @pl.when((j == 2) & (half == 0))
        def _():
            resid[seq] = ml[3]

        @pl.when((j == 2) & (half == 1))
        def _():
            resid[seq] = mr[3]

    def store(n, columns, value):
        for k, ref in enumerate((own, plus, minus)):
            for seq in range(2):
                at = (k * 2 + seq) * TILE
                ref[seq, n, :, columns] = value[at : at + TILE]

    down(z, lambda: hid[0:6].reshape(6 * TILE, 2 * UNITS), downs, store)


VMEM = pl.BlockSpec(memory_space=pltpu.VMEM)
SMEM = pl.BlockSpec(memory_space=pltpu.SMEM)


def call(kernel, out_shape, scratch, flops, *operands):
    return pl.pallas_call(
        kernel,
        in_specs=[SMEM] + [VMEM] * (len(operands) - 1),
        out_specs=[VMEM] * len(out_shape),
        out_shape=out_shape,
        scratch_shapes=scratch,
        compiler_params=pltpu.CompilerParams(vmem_limit_bytes=LIMIT * MIB),
        cost_estimate=pl.CostEstimate(flops=flops // COST, bytes_accessed=BYTES, transcendentals=0),
    )(*operands)


def load_kernel(own, other, after, out, token, sems):
    del after
    copies = [pltpu.make_async_copy(ref, out.at[i], sems.at[i]) for i, ref in enumerate((own, other))]
    for copy in copies:
        copy.start()
    token[...] = jnp.zeros_like(token)
    for copy in copies:
        copy.wait()


def loaded(own, other, after):
    return pl.pallas_call(
        load_kernel,
        in_specs=[pl.BlockSpec(memory_space=pltpu.HBM)] * 2 + [pl.BlockSpec(memory_space=pl.ANY)],
        out_specs=[VMEM, VMEM],
        out_shape=[pltpu.VMEM((2, *own.shape), own.dtype), jax.ShapeDtypeStruct((8, 128), jnp.float32)],
        scratch_shapes=[pltpu.SemaphoreType.DMA((2,))],
        compiler_params=pltpu.CompilerParams(vmem_limit_bytes=LIMIT * MIB),
        cost_estimate=pl.CostEstimate(flops=0, bytes_accessed=16 * MIB, transcendentals=0),
    )(own, other, after)


def compute(place, far_place, near, block, xm, xp, ml, mr, gain, bias, b_all, ups, downs):
    mul = 2 * 2 * UNITS * RING * PART
    far = call(
        far_kernel,
        [jax.ShapeDtypeStruct((RING, TILE, PART), jnp.bfloat16)] * 2
        + [jax.ShapeDtypeStruct((8, TILE, 2 * UNITS), jnp.bfloat16)],
        [pltpu.VMEM((RING, 2 * TILE, PART), jnp.bfloat16)],
        4 * TILE * mul,
        far_place, ml, mr, gain, bias, b_all, near, ups, downs,
    )
    rest = call(
        rest_kernel,
        [jax.ShapeDtypeStruct((2, RING, TILE, PART), jnp.bfloat16)] * 3
        + [jax.ShapeDtypeStruct((2, TILE, PART), jnp.bfloat16)],
        [],
        6 * TILE * mul,
        place, far[2], downs, block, xm, ml, mr, xp,
    )
    return far[:2], rest


def shards(acts, ln_gain, ln_bias, w_up, b_up, w_down, b_down):
    x, z, core = (lax.axis_index(a) for a in ("x", "zh", "core"))
    place = jnp.stack([x, z]).astype(jnp.int32)
    up_o, down_o = w_up[0], w_down[0]
    gain, bias = ln_gain[0].reshape(RING, PART), ln_bias[0].reshape(RING, PART)

    split = acts[0].reshape(2, 2, TILE, HALF)
    got, b_up_s = lax.optimization_barrier((swapped(acts[0]), swapped(b_up)))
    mine = lax.dynamic_index_in_dim(split, core, 1, keepdims=False)
    got = lax.dynamic_index_in_dim(got.reshape(2, 2, TILE, HALF), core, 1, keepdims=False)
    low = jnp.where(core == 0, mine, got)
    high = jnp.where(core == 0, got, mine)
    block = jnp.concatenate([low, high], axis=-1)
    block, up_o = lax.optimization_barrier((block, up_o))
    b_all = jnp.concatenate([b_up, b_up_s], axis=0)

    zp, zm = sent(block, "zh", 1), sent(block, "zh", -1)
    xp, xm = sent(block, "x", 1), sent(block, "x", -1)
    up_s = swapped(up_o)
    zp, zm, xp, xm, up_s, down_o = lax.optimization_barrier((zp, zm, xp, xm, up_s, down_o))
    zs = jnp.stack([zp, zm])
    sp, sm = sent(zs, "x", 1), sent(zs, "x", -1)
    za, zb = sent(zp[0], "zh", 1), sent(zm[1], "zh", -1)
    za, zb = lax.optimization_barrier((za, zb))
    zz = jnp.stack([za, zb])
    qp, qm = sent(zz, "x", 1), sent(zz, "x", -1)
    down_s = swapped(down_o)
    ups, token = loaded(up_o, up_s, b_all)
    sp, sm, qp, qm, xp, xm, token = lax.optimization_barrier((sp, sm, qp, qm, xp, xm, token))
    place = place + token[0, :2].astype(jnp.int32)
    ml = sent(jnp.stack([sp[0, 0], sp[1, 0], qp[0], xp[0]]), "x", 1)
    mr = sent(jnp.stack([sm[0, 1], sm[1, 1], qm[1], xm[1]]), "x", -1)
    near = call(
        near_kernel,
        [jax.ShapeDtypeStruct((6, TILE, 2 * UNITS), jnp.bfloat16)],
        [pltpu.VMEM((RING, 6 * TILE, PART), jnp.bfloat16)],
        6 * TILE * 4 * UNITS * RING * PART,
        place, block, zs, zz, xm, sm, qm, xp, sp, qp, gain, bias, b_all, ups,
    )[0]
    downs, token = loaded(down_o, down_s, near)
    far_place = place + token[0, :2].astype(jnp.int32)

    (far_l, far_r), (own, plus, minus, resid) = compute(
        place, far_place, near, block, xm, xp, ml, mr, gain, bias, b_all, ups, downs
    )
    l, r = lax.optimization_barrier((sent(far_l, "x", 1), sent(far_r, "x", -1)))

    def over_x(first, last):
        to_left = jnp.stack([added(plus[0, first:last], l[first:last]), plus[1, first:last]])
        to_right = jnp.stack([minus[0, first:last], added(minus[1, first:last], r[first:last])])
        return lax.optimization_barrier((sent(to_left, "x", 1), sent(to_right, "x", -1)))

    fl2, fr2 = over_x(0, 1)
    fl1, fr1 = over_x(1, 3)
    fl0, fr0 = over_x(3, 4)
    s2 = added(own[:, 0], fl2[:, 0], fr2[:, 0])
    zl, zr = lax.optimization_barrier((sent(s2[0], "zh", 1), sent(s2[1], "zh", -1)))
    t = added(own[:, 1:3], fl1, fr1)
    zfl = sent(jnp.stack([added(t[0, 0], zl), t[1, 0]]), "zh", 1)
    zfr = sent(jnp.stack([t[0, 1], added(t[1, 1], zr)]), "zh", -1)
    zfl, zfr, fl0, fr0 = lax.optimization_barrier((zfl, zfr, fl0, fr0))
    shift = lax.dynamic_slice_in_dim(b_down[0], z * PART, PART, 0)
    value = added(own[:, 3], fl0[:, 0], fr0[:, 0], zfl, zfr, resid, shift)
    low, high = value[..., :HALF], value[..., HALF:]
    keep = next_section(jnp.where(core == 0, low, high), 0)
    cross = next_section(jnp.where(core == 0, high, low), 1)
    out = jnp.stack([jnp.where(core == 0, keep, cross), jnp.where(core == 0, cross, keep)], axis=1)
    return out.reshape(1, BATCH, 2 * TILE, HALF)


def solution(mesh):
    fine = Mesh(mesh.devices.reshape(4, 2, 4, 4, 2), ("y", "zl", "x", "zh", "core"))
    section, rows, hid = ("y", "zl"), "x", ("zh", "core")
    in_specs = (
        P(section, rows, hid),
        P(section, None),
        P(section, None),
        P(section, None, ("x", "zh", "core")),
        P(section, ("x", "zh", "core")),
        P(section, ("x", "zh", "core"), None),
        P(section, None),
    )
    out_specs = P(section, None, rows, hid)
    return jax.shard_map(shards, mesh=fine, in_specs=in_specs, out_specs=out_specs, check_vma=False)
```

```python
import jax
import jax.numpy as jnp
from jax import lax
from jax.experimental import pallas as pl
from jax.experimental.pallas import tpu as pltpu
from jax.sharding import Mesh
from jax.sharding import PartitionSpec as P

BATCH = 2
RING = 4
TILE = 64
PART = 1024
HALF = PART // 2
UNITS = 512
STEP = 256
ROWS = 16
UNROLL = 4
EPS = 1e-05
MIB = 1024 * 1024
LIMIT = 8
COST = 4
BYTES = MIB


def sent(block, axis, distance):
    return lax.ppermute(block, axis, [(i, (i + distance) % RING) for i in range(RING)])


def swapped(block):
    return lax.ppermute(block, "core", [(0, 1), (1, 0)])


def next_section(block, cross):
    pairs = []
    for section in range(8):
        for core in range(2):
            pairs.append((section * 2 + core, (section + 1) % 8 * 2 + (core ^ cross)))
    return lax.ppermute(block, ("y", "zl", "core"), pairs)


def added(*terms):
    return sum(t.astype(jnp.float32) for t in terms).astype(jnp.bfloat16)


def normalize(pieces, z, gain, bias, normed, at, rows):
    def some(i, _):
        start = pl.multiple_of(i * ROWS, ROWS)
        values = [read(start).astype(jnp.float32) for read in pieces]
        mean = sum(jnp.sum(v, axis=-1, keepdims=True) for v in values) / (RING * PART)
        centered = [v - mean for v in values]
        spread = sum(jnp.sum(v * v, axis=-1, keepdims=True) for v in centered) / (RING * PART)
        scale = lax.rsqrt(spread + EPS)
        for k in range(RING):
            true = (z + k) & 3
            value = centered[k] * scale * gain[pl.ds(true, 1), :] + bias[pl.ds(true, 1), :]
            normed[true, pl.ds(at + start, ROWS), :] = value.astype(jnp.bfloat16)
        return 0

    lax.fori_loop(0, rows // ROWS, some, 0, unroll=UNROLL)


def reader(ref, *lead):
    return lambda start: ref[(*lead, pl.ds(start, ROWS), slice(None))]


def halves(ref, *lead):
    return lambda start: ref[(*lead, start // TILE, pl.ds(pl.multiple_of(start % TILE, ROWS), ROWS), slice(None))]


def up(normed, ups, b_up, store, unroll=1):
    def some(n, _):
        columns = pl.ds(pl.multiple_of((n & 1) * STEP, STEP), STEP)
        pre = b_up[pl.ds(n >> 1, 1), columns]
        for k in range(RING):
            pre = pre + jnp.dot(
                normed[k], ups[n >> 1, pl.ds(k * PART, PART), columns], preferred_element_type=jnp.float32
            )
        store(pl.ds(pl.multiple_of(n * STEP, STEP), STEP), jax.nn.gelu(pre, approximate=True).astype(jnp.bfloat16))
        return 0

    lax.fori_loop(0, 2 * UNITS // STEP, some, 0, unroll=unroll)


def near_kernel(place, block, zs, zz, xm, sm, qm, xp, sp, qp, gain, bias, b_up, ups, hidden, normed):
    z = place[1]
    for slot, (a, b, c) in enumerate(((block, zs, zz), (xm, sm, qm), (xp, sp, qp))):
        pieces = [halves(a), halves(b, 1), halves(c), halves(b, 0)]
        normalize(pieces, z, gain, bias, normed, slot * 2 * TILE, 2 * TILE)

    def store(columns, value):
        for tile in range(6):
            hidden[tile, :, columns] = value[tile * TILE : (tile + 1) * TILE]

    up(normed, ups, b_up, store)


def down(z, rows, downs, store, wide=HALF, unroll=1):
    each = PART // wide

    def some(i, _):
        n, t = i // each, i % each
        k = jnp.where(n == 0, 2, jnp.where(n == 3, 0, 2 * n - 1))
        start = pl.ds(pl.multiple_of(((z + k) & 3) * PART + t * wide, wide), wide)
        value = rows()
        term = jnp.dot(value[:, :UNITS], downs[0, :, start], preferred_element_type=jnp.float32)
        term = term + jnp.dot(value[:, UNITS:], downs[1, :, start], preferred_element_type=jnp.float32)
        store(n, pl.ds(pl.multiple_of(t * wide, wide), wide), term.astype(jnp.bfloat16))
        return 0

    lax.fori_loop(0, RING * each, some, 0, unroll=unroll)


def far_kernel(place, ml, mr, gain, bias, b_up, near, ups, downs, plus, minus, hid, normed):
    x, z = place[0], place[1]

    def home(j, half):
        row = (x + j) & 3
        dest = ((row & 1) * 2 + half - x) & 3
        return (dest ^ (dest >> 1)) * 2 + (row >> 1)

    for half, a in enumerate((ml, mr)):
        pieces = [reader(a, 3), reader(a, 1), reader(a, 2), reader(a, 0)]
        normalize(pieces, z, gain, bias, normed, half * TILE, TILE)
    for slot, j in enumerate((0, 1, 3)):
        for half in range(2):
            hid[home(j, half)] = near[slot * 2 + half]

    def store(columns, value):
        for half in range(2):
            hid[home(2, half), :, columns] = value[half * TILE : (half + 1) * TILE]

    up(normed, ups, b_up, store, unroll=4)

    def send(n, columns, value):
        plus[n, :, columns] = value[:TILE]
        minus[n, :, columns] = value[TILE:]

    down(z, lambda: hid[6:8].reshape(2 * TILE, 2 * UNITS), downs, send, unroll=4)


def rest_kernel(place, hid, downs, block, xm, ml, mr, xp, own, plus, minus, resid):
    x, z = place[0], place[1]
    for seq in range(2):
        row, half = 2 * seq + (x >> 1), x & 1
        j = (row - x) & 3
        for at, ref in ((0, block), (1, xm), (3, xp)):

            @pl.when(j == at)
            def _(ref=ref):
                resid[seq] = ref[half]

        @pl.when((j == 2) & (half == 0))
        def _():
            resid[seq] = ml[3]

        @pl.when((j == 2) & (half == 1))
        def _():
            resid[seq] = mr[3]

    def store(n, columns, value):
        for k, ref in enumerate((own, plus, minus)):
            for seq in range(2):
                at = (k * 2 + seq) * TILE
                ref[seq, n, :, columns] = value[at : at + TILE]

    down(z, lambda: hid[0:6].reshape(6 * TILE, 2 * UNITS), downs, store)


VMEM = pl.BlockSpec(memory_space=pltpu.VMEM)
SMEM = pl.BlockSpec(memory_space=pltpu.SMEM)


def call(kernel, out_shape, scratch, flops, *operands):
    return pl.pallas_call(
        kernel,
        in_specs=[SMEM] + [VMEM] * (len(operands) - 1),
        out_specs=[VMEM] * len(out_shape),
        out_shape=out_shape,
        scratch_shapes=scratch,
        compiler_params=pltpu.CompilerParams(vmem_limit_bytes=LIMIT * MIB),
        cost_estimate=pl.CostEstimate(flops=flops // COST, bytes_accessed=BYTES, transcendentals=0),
    )(*operands)


def load_kernel(own, other, after, out, token, sems):
    del after
    copies = [pltpu.make_async_copy(ref, out.at[i], sems.at[i]) for i, ref in enumerate((own, other))]
    for copy in copies:
        copy.start()
    token[...] = jnp.zeros_like(token)
    for copy in copies:
        copy.wait()


def loaded(own, other, after):
    return pl.pallas_call(
        load_kernel,
        in_specs=[pl.BlockSpec(memory_space=pltpu.HBM)] * 2 + [pl.BlockSpec(memory_space=pl.ANY)],
        out_specs=[VMEM, VMEM],
        out_shape=[pltpu.VMEM((2, *own.shape), own.dtype), jax.ShapeDtypeStruct((8, 128), jnp.float32)],
        scratch_shapes=[pltpu.SemaphoreType.DMA((2,))],
        compiler_params=pltpu.CompilerParams(vmem_limit_bytes=LIMIT * MIB),
        cost_estimate=pl.CostEstimate(flops=0, bytes_accessed=16 * MIB, transcendentals=0),
    )(own, other, after)


def compute(place, far_place, near, block, xm, xp, ml, mr, gain, bias, b_all, ups, downs):
    mul = 2 * 2 * UNITS * RING * PART
    far = call(
        far_kernel,
        [jax.ShapeDtypeStruct((RING, TILE, PART), jnp.bfloat16)] * 2
        + [jax.ShapeDtypeStruct((8, TILE, 2 * UNITS), jnp.bfloat16)],
        [pltpu.VMEM((RING, 2 * TILE, PART), jnp.bfloat16)],
        4 * TILE * mul,
        far_place, ml, mr, gain, bias, b_all, near, ups, downs,
    )
    rest = call(
        rest_kernel,
        [jax.ShapeDtypeStruct((2, RING, TILE, PART), jnp.bfloat16)] * 3
        + [jax.ShapeDtypeStruct((2, TILE, PART), jnp.bfloat16)],
        [],
        6 * TILE * mul,
        place, far[2], downs, block, xm, ml, mr, xp,
    )
    return far[:2], rest


def shards(acts, ln_gain, ln_bias, w_up, b_up, w_down, b_down):
    x, z, core = (lax.axis_index(a) for a in ("x", "zh", "core"))
    place = jnp.stack([x, z]).astype(jnp.int32)
    up_o, down_o = w_up[0], w_down[0]
    gain, bias = ln_gain[0].reshape(RING, PART), ln_bias[0].reshape(RING, PART)

    split = acts[0].reshape(2, 2, TILE, HALF)
    got, b_up_s, up_o = lax.optimization_barrier((swapped(acts[0]), swapped(b_up), up_o))
    mine = lax.dynamic_index_in_dim(split, core, 1, keepdims=False)
    got = lax.dynamic_index_in_dim(got.reshape(2, 2, TILE, HALF), core, 1, keepdims=False)
    low = jnp.where(core == 0, mine, got)
    high = jnp.where(core == 0, got, mine)
    block = jnp.concatenate([low, high], axis=-1)
    b_all = jnp.concatenate([b_up, b_up_s], axis=0)

    zp, zm = sent(block, "zh", 1), sent(block, "zh", -1)
    xp, xm = sent(block, "x", 1), sent(block, "x", -1)
    up_s = swapped(up_o)
    zp, zm, xp, xm, up_s, down_o = lax.optimization_barrier((zp, zm, xp, xm, up_s, down_o))
    zs = jnp.stack([zp, zm])
    sp, sm = sent(zs, "x", 1), sent(zs, "x", -1)
    za, zb = sent(zp[0], "zh", 1), sent(zm[1], "zh", -1)
    za, zb = lax.optimization_barrier((za, zb))
    zz = jnp.stack([za, zb])
    qp, qm = sent(zz, "x", 1), sent(zz, "x", -1)
    down_s = swapped(down_o)
    ups, token = loaded(up_o, up_s, b_all)
    sp, sm, qp, qm, xp, xm, token = lax.optimization_barrier((sp, sm, qp, qm, xp, xm, token))
    place = place + token[0, :2].astype(jnp.int32)
    ml = sent(jnp.stack([sp[0, 0], sp[1, 0], qp[0], xp[0]]), "x", 1)
    mr = sent(jnp.stack([sm[0, 1], sm[1, 1], qm[1], xm[1]]), "x", -1)
    near = call(
        near_kernel,
        [jax.ShapeDtypeStruct((6, TILE, 2 * UNITS), jnp.bfloat16)],
        [pltpu.VMEM((RING, 6 * TILE, PART), jnp.bfloat16)],
        6 * TILE * 4 * UNITS * RING * PART,
        place, block, zs, zz, xm, sm, qm, xp, sp, qp, gain, bias, b_all, ups,
    )[0]
    downs, token = loaded(down_o, down_s, near)
    far_place = place + token[0, :2].astype(jnp.int32)

    (far_l, far_r), (own, plus, minus, resid) = compute(
        place, far_place, near, block, xm, xp, ml, mr, gain, bias, b_all, ups, downs
    )
    l, r = lax.optimization_barrier((sent(far_l, "x", 1), sent(far_r, "x", -1)))

    def over_x(first, last):
        to_left = jnp.stack([added(plus[0, first:last], l[first:last]), plus[1, first:last]])
        to_right = jnp.stack([minus[0, first:last], added(minus[1, first:last], r[first:last])])
        return lax.optimization_barrier((sent(to_left, "x", 1), sent(to_right, "x", -1)))

    fl2, fr2 = over_x(0, 1)
    fl1, fr1 = over_x(1, 3)
    fl0, fr0 = over_x(3, 4)
    s2 = added(own[:, 0], fl2[:, 0], fr2[:, 0])
    zl, zr = lax.optimization_barrier((sent(s2[0], "zh", 1), sent(s2[1], "zh", -1)))
    t = added(own[:, 1:3], fl1, fr1)
    zfl = sent(jnp.stack([added(t[0, 0], zl), t[1, 0]]), "zh", 1)
    zfr = sent(jnp.stack([t[0, 1], added(t[1, 1], zr)]), "zh", -1)
    zfl, zfr, fl0, fr0 = lax.optimization_barrier((zfl, zfr, fl0, fr0))
    shift = lax.dynamic_slice_in_dim(b_down[0], z * PART, PART, 0)
    value = added(own[:, 3], fl0[:, 0], fr0[:, 0], zfl, zfr, resid, shift)
    low, high = value[..., :HALF], value[..., HALF:]
    keep = next_section(jnp.where(core == 0, low, high), 0)
    cross = next_section(jnp.where(core == 0, high, low), 1)
    out = jnp.stack([jnp.where(core == 0, keep, cross), jnp.where(core == 0, cross, keep)], axis=1)
    return out.reshape(1, BATCH, 2 * TILE, HALF)


def solution(mesh):
    fine = Mesh(mesh.devices.reshape(4, 2, 4, 4, 2), ("y", "zl", "x", "zh", "core"))
    section, rows, hid = ("y", "zl"), "x", ("zh", "core")
    in_specs = (
        P(section, rows, hid),
        P(section, None),
        P(section, None),
        P(section, None, ("x", "zh", "core")),
        P(section, ("x", "zh", "core")),
        P(section, ("x", "zh", "core"), None),
        P(section, None),
    )
    out_specs = P(section, None, rows, hid)
    return jax.shard_map(shards, mesh=fine, in_specs=in_specs, out_specs=out_specs, check_vma=False)
```

```python
import jax
import jax.numpy as jnp
from jax import lax
from jax.experimental import pallas as pl
from jax.experimental.pallas import tpu as pltpu
from jax.sharding import Mesh
from jax.sharding import PartitionSpec as P

BATCH = 2
RING = 4
TILE = 64
PART = 1024
HALF = PART // 2
UNITS = 512
STEP = 256
ROWS = 16
UNROLL = 4
EPS = 1e-05
MIB = 1024 * 1024
LIMIT = 8
COST = 4
BYTES = MIB


def sent(block, axis, distance):
    return lax.ppermute(block, axis, [(i, (i + distance) % RING) for i in range(RING)])


def swapped(block):
    return lax.ppermute(block, "core", [(0, 1), (1, 0)])


def next_section(block, cross):
    pairs = []
    for section in range(8):
        for core in range(2):
            pairs.append((section * 2 + core, (section + 1) % 8 * 2 + (core ^ cross)))
    return lax.ppermute(block, ("y", "zl", "core"), pairs)


def added(*terms):
    return sum(t.astype(jnp.float32) for t in terms).astype(jnp.bfloat16)


def normalize(pieces, z, gain, bias, normed, at, rows):
    def some(i, _):
        start = pl.multiple_of(i * ROWS, ROWS)
        values = [read(start).astype(jnp.float32) for read in pieces]
        mean = sum(jnp.sum(v, axis=-1, keepdims=True) for v in values) / (RING * PART)
        centered = [v - mean for v in values]
        spread = sum(jnp.sum(v * v, axis=-1, keepdims=True) for v in centered) / (RING * PART)
        scale = lax.rsqrt(spread + EPS)
        for k in range(RING):
            true = (z + k) & 3
            value = centered[k] * scale * gain[pl.ds(true, 1), :] + bias[pl.ds(true, 1), :]
            normed[true, pl.ds(at + start, ROWS), :] = value.astype(jnp.bfloat16)
        return 0

    lax.fori_loop(0, rows // ROWS, some, 0, unroll=UNROLL)


def reader(ref, *lead):
    return lambda start: ref[(*lead, pl.ds(start, ROWS), slice(None))]


def halves(ref, *lead):
    return lambda start: ref[(*lead, start // TILE, pl.ds(pl.multiple_of(start % TILE, ROWS), ROWS), slice(None))]


def up(normed, ups, b_up, store, unroll=1):
    def some(n, _):
        columns = pl.ds(pl.multiple_of((n & 1) * STEP, STEP), STEP)
        pre = b_up[pl.ds(n >> 1, 1), columns]
        for k in range(RING):
            pre = pre + jnp.dot(
                normed[k], ups[n >> 1, pl.ds(k * PART, PART), columns], preferred_element_type=jnp.float32
            )
        store(pl.ds(pl.multiple_of(n * STEP, STEP), STEP), jax.nn.gelu(pre, approximate=True).astype(jnp.bfloat16))
        return 0

    lax.fori_loop(0, 2 * UNITS // STEP, some, 0, unroll=unroll)


def near_kernel(place, block, zs, zz, xm, sm, qm, xp, sp, qp, gain, bias, b_up, ups, hidden, normed):
    z = place[1]
    for slot, (a, b, c) in enumerate(((block, zs, zz), (xm, sm, qm), (xp, sp, qp))):
        pieces = [halves(a), halves(b, 1), halves(c), halves(b, 0)]
        normalize(pieces, z, gain, bias, normed, slot * 2 * TILE, 2 * TILE)

    def store(columns, value):
        for tile in range(6):
            hidden[tile, :, columns] = value[tile * TILE : (tile + 1) * TILE]

    up(normed, ups, b_up, store)


def down(z, rows, downs, store, wide=HALF, unroll=1):
    each = PART // wide

    def some(i, _):
        n, t = i // each, i % each
        k = jnp.where(n == 0, 2, jnp.where(n == 3, 0, 2 * n - 1))
        start = pl.ds(pl.multiple_of(((z + k) & 3) * PART + t * wide, wide), wide)
        value = rows()
        term = jnp.dot(value[:, :UNITS], downs[0, :, start], preferred_element_type=jnp.float32)
        term = term + jnp.dot(value[:, UNITS:], downs[1, :, start], preferred_element_type=jnp.float32)
        store(n, pl.ds(pl.multiple_of(t * wide, wide), wide), term.astype(jnp.bfloat16))
        return 0

    lax.fori_loop(0, RING * each, some, 0, unroll=unroll)


def far_kernel(place, ml, mr, gain, bias, b_up, near, ups, downs, plus, minus, hid, normed):
    x, z = place[0], place[1]

    def home(j, half):
        row = (x + j) & 3
        dest = ((row & 1) * 2 + half - x) & 3
        return (dest ^ (dest >> 1)) * 2 + (row >> 1)

    for half, a in enumerate((ml, mr)):
        pieces = [reader(a, 3), reader(a, 1), reader(a, 2), reader(a, 0)]
        normalize(pieces, z, gain, bias, normed, half * TILE, TILE)
    for slot, j in enumerate((0, 1, 3)):
        for half in range(2):
            hid[home(j, half)] = near[slot * 2 + half]

    def store(columns, value):
        for half in range(2):
            hid[home(2, half), :, columns] = value[half * TILE : (half + 1) * TILE]

    up(normed, ups, b_up, store, unroll=4)

    def send(n, columns, value):
        plus[n, :, columns] = value[:TILE]
        minus[n, :, columns] = value[TILE:]

    down(z, lambda: hid[6:8].reshape(2 * TILE, 2 * UNITS), downs, send, wide=PART, unroll=4)


def rest_kernel(place, hid, downs, block, xm, ml, mr, xp, own, plus, minus, resid):
    x, z = place[0], place[1]
    for seq in range(2):
        row, half = 2 * seq + (x >> 1), x & 1
        j = (row - x) & 3
        for at, ref in ((0, block), (1, xm), (3, xp)):

            @pl.when(j == at)
            def _(ref=ref):
                resid[seq] = ref[half]

        @pl.when((j == 2) & (half == 0))
        def _():
            resid[seq] = ml[3]

        @pl.when((j == 2) & (half == 1))
        def _():
            resid[seq] = mr[3]

    def store(n, columns, value):
        for k, ref in enumerate((own, plus, minus)):
            for seq in range(2):
                at = (k * 2 + seq) * TILE
                ref[seq, n, :, columns] = value[at : at + TILE]

    down(z, lambda: hid[0:6].reshape(6 * TILE, 2 * UNITS), downs, store)


VMEM = pl.BlockSpec(memory_space=pltpu.VMEM)
SMEM = pl.BlockSpec(memory_space=pltpu.SMEM)


def call(kernel, out_shape, scratch, flops, *operands):
    return pl.pallas_call(
        kernel,
        in_specs=[SMEM] + [VMEM] * (len(operands) - 1),
        out_specs=[VMEM] * len(out_shape),
        out_shape=out_shape,
        scratch_shapes=scratch,
        compiler_params=pltpu.CompilerParams(vmem_limit_bytes=LIMIT * MIB),
        cost_estimate=pl.CostEstimate(flops=flops // COST, bytes_accessed=BYTES, transcendentals=0),
    )(*operands)


def load_kernel(own, other, after, out, token, sems):
    del after
    copies = [pltpu.make_async_copy(ref, out.at[i], sems.at[i]) for i, ref in enumerate((own, other))]
    for copy in copies:
        copy.start()
    token[...] = jnp.zeros_like(token)
    for copy in copies:
        copy.wait()


def loaded(own, other, after):
    return pl.pallas_call(
        load_kernel,
        in_specs=[pl.BlockSpec(memory_space=pltpu.HBM)] * 2 + [pl.BlockSpec(memory_space=pl.ANY)],
        out_specs=[VMEM, VMEM],
        out_shape=[pltpu.VMEM((2, *own.shape), own.dtype), jax.ShapeDtypeStruct((8, 128), jnp.float32)],
        scratch_shapes=[pltpu.SemaphoreType.DMA((2,))],
        compiler_params=pltpu.CompilerParams(vmem_limit_bytes=LIMIT * MIB),
        cost_estimate=pl.CostEstimate(flops=0, bytes_accessed=16 * MIB, transcendentals=0),
    )(own, other, after)


def compute(place, far_place, near, block, xm, xp, ml, mr, gain, bias, b_all, ups, downs):
    mul = 2 * 2 * UNITS * RING * PART
    far = call(
        far_kernel,
        [jax.ShapeDtypeStruct((RING, TILE, PART), jnp.bfloat16)] * 2
        + [jax.ShapeDtypeStruct((8, TILE, 2 * UNITS), jnp.bfloat16)],
        [pltpu.VMEM((RING, 2 * TILE, PART), jnp.bfloat16)],
        4 * TILE * mul,
        far_place, ml, mr, gain, bias, b_all, near, ups, downs,
    )
    rest = call(
        rest_kernel,
        [jax.ShapeDtypeStruct((2, RING, TILE, PART), jnp.bfloat16)] * 3
        + [jax.ShapeDtypeStruct((2, TILE, PART), jnp.bfloat16)],
        [],
        6 * TILE * mul,
        place, far[2], downs, block, xm, ml, mr, xp,
    )
    return far[:2], rest


def shards(acts, ln_gain, ln_bias, w_up, b_up, w_down, b_down):
    x, z, core = (lax.axis_index(a) for a in ("x", "zh", "core"))
    place = jnp.stack([x, z]).astype(jnp.int32)
    up_o, down_o = w_up[0], w_down[0]
    gain, bias = ln_gain[0].reshape(RING, PART), ln_bias[0].reshape(RING, PART)

    split = acts[0].reshape(2, 2, TILE, HALF)
    got, b_up_s, up_o = lax.optimization_barrier((swapped(acts[0]), swapped(b_up), up_o))
    mine = lax.dynamic_index_in_dim(split, core, 1, keepdims=False)
    got = lax.dynamic_index_in_dim(got.reshape(2, 2, TILE, HALF), core, 1, keepdims=False)
    low = jnp.where(core == 0, mine, got)
    high = jnp.where(core == 0, got, mine)
    block = jnp.concatenate([low, high], axis=-1)
    b_all = jnp.concatenate([b_up, b_up_s], axis=0)

    zp, zm = sent(block, "zh", 1), sent(block, "zh", -1)
    xp, xm = sent(block, "x", 1), sent(block, "x", -1)
    up_s = swapped(up_o)
    zp, zm, xp, xm, up_s, down_o = lax.optimization_barrier((zp, zm, xp, xm, up_s, down_o))
    zs = jnp.stack([zp, zm])
    sp, sm = sent(zs, "x", 1), sent(zs, "x", -1)
    za, zb = sent(zp[0], "zh", 1), sent(zm[1], "zh", -1)
    za, zb = lax.optimization_barrier((za, zb))
    zz = jnp.stack([za, zb])
    qp, qm = sent(zz, "x", 1), sent(zz, "x", -1)
    down_s = swapped(down_o)
    ups, token = loaded(up_o, up_s, b_all)
    sp, sm, qp, qm, xp, xm, token = lax.optimization_barrier((sp, sm, qp, qm, xp, xm, token))
    place = place + token[0, :2].astype(jnp.int32)
    ml = sent(jnp.stack([sp[0, 0], sp[1, 0], qp[0], xp[0]]), "x", 1)
    mr = sent(jnp.stack([sm[0, 1], sm[1, 1], qm[1], xm[1]]), "x", -1)
    near = call(
        near_kernel,
        [jax.ShapeDtypeStruct((6, TILE, 2 * UNITS), jnp.bfloat16)],
        [pltpu.VMEM((RING, 6 * TILE, PART), jnp.bfloat16)],
        6 * TILE * 4 * UNITS * RING * PART,
        place, block, zs, zz, xm, sm, qm, xp, sp, qp, gain, bias, b_all, ups,
    )[0]
    downs, token = loaded(down_o, down_s, near)
    far_place = place + token[0, :2].astype(jnp.int32)

    (far_l, far_r), (own, plus, minus, resid) = compute(
        place, far_place, near, block, xm, xp, ml, mr, gain, bias, b_all, ups, downs
    )
    l, r = lax.optimization_barrier((sent(far_l, "x", 1), sent(far_r, "x", -1)))

    def over_x(first, last):
        to_left = jnp.stack([added(plus[0, first:last], l[first:last]), plus[1, first:last]])
        to_right = jnp.stack([minus[0, first:last], added(minus[1, first:last], r[first:last])])
        return lax.optimization_barrier((sent(to_left, "x", 1), sent(to_right, "x", -1)))

    fl2, fr2 = over_x(0, 1)
    fl1, fr1 = over_x(1, 3)
    fl0, fr0 = over_x(3, 4)
    s2 = added(own[:, 0], fl2[:, 0], fr2[:, 0])
    zl, zr = lax.optimization_barrier((sent(s2[0], "zh", 1), sent(s2[1], "zh", -1)))
    t = added(own[:, 1:3], fl1, fr1)
    zfl = sent(jnp.stack([added(t[0, 0], zl), t[1, 0]]), "zh", 1)
    zfr = sent(jnp.stack([t[0, 1], added(t[1, 1], zr)]), "zh", -1)
    zfl, zfr, fl0, fr0 = lax.optimization_barrier((zfl, zfr, fl0, fr0))
    shift = lax.dynamic_slice_in_dim(b_down[0], z * PART, PART, 0)
    value = added(own[:, 3], fl0[:, 0], fr0[:, 0], zfl, zfr, resid, shift)
    low, high = value[..., :HALF], value[..., HALF:]
    keep = next_section(jnp.where(core == 0, low, high), 0)
    cross = next_section(jnp.where(core == 0, high, low), 1)
    out = jnp.stack([jnp.where(core == 0, keep, cross), jnp.where(core == 0, cross, keep)], axis=1)
    return out.reshape(1, BATCH, 2 * TILE, HALF)


def solution(mesh):
    fine = Mesh(mesh.devices.reshape(4, 2, 4, 4, 2), ("y", "zl", "x", "zh", "core"))
    section, rows, hid = ("y", "zl"), "x", ("zh", "core")
    in_specs = (
        P(section, rows, hid),
        P(section, None),
        P(section, None),
        P(section, None, ("x", "zh", "core")),
        P(section, ("x", "zh", "core")),
        P(section, ("x", "zh", "core"), None),
        P(section, None),
    )
    out_specs = P(section, None, rows, hid)
    return jax.shard_map(shards, mesh=fine, in_specs=in_specs, out_specs=out_specs, check_vma=False)
```
